128 devices in a mesh: grp: 8 (over x, y_hi), seq: 16 (over y_lo, z, core).
Axes of the slice: x: 4, y: 4 (y_hi: 2, y_lo: 2; y = y_hi * 2 + y_lo), z: 4, core: 2. Of those that a mesh axis runs over, the one named last changes fastest.
Arguments:
- queries: bfloat16 [32768, 4096], P(('grp', 'seq')), parts along dimension 0, may hold values from -200 to 200
- keys_resp: bfloat16 [32768, 512], P(('grp', 'seq')), parts along dimension 0, may hold values from -6 to 6
- values_resp: bfloat16 [32768, 512], P(('grp', 'seq')), parts along dimension 0, may hold values from -12 to 12
- keys_prompt: bfloat16 [8192, 512], P(('grp', 'seq')), parts along dimension 0, may hold values from -6 to 6
- values_prompt: bfloat16 [8192, 512], P(('grp', 'seq')), parts along dimension 0, may hold values from -12 to 12
- grad_out: bfloat16 [32768, 4096], P(('grp', 'seq')), parts along dimension 0, may hold values from -48 to 48
- resp_len: int32 [128], P(('grp', 'seq')), parts along dimension 0, may hold values from 128 to 256, as said below
Outputs:
- grad_queries: bfloat16 [32768, 4096], P(('grp', 'seq')), parts along dimension 0
- grad_keys_resp: bfloat16 [32768, 512], P(('grp', 'seq')), parts along dimension 0
- grad_values_resp: bfloat16 [32768, 512], P(('grp', 'seq')), parts along dimension 0
- grad_keys_prompt: bfloat16 [8192, 512], P(('grp', 'seq')), parts along dimension 0
- grad_values_prompt: bfloat16 [8192, 512], P(('grp', 'seq')), parts along dimension 0
The draws below stay inside these ranges and needn't reach their ends.
There are 8 independent parts, one for each index of `grp`. The reference program is written for one: setup_inputs(seed, part) draws one part's arguments, and reference() takes and returns one part's arrays. A program takes and returns all parts, laid end to end along the dimension named above; each array names one. Nothing has to cross between parts.
Inputs may be any that keep to these rules, and one draw needn't show every extreme that they name: `resp_len`: each length is a multiple of 128; in every group some rollout has length 256.
All inputs are finite; a program needn't handle non-finite values.
Results may differ from the reference program's by a relative error of at most 0.022.
Values may be sent and summed in bfloat16 or wider, within the bound.
A program may use at most 128 MiB of HBM per device.

```python
import jax
import jax.numpy as jnp
from jax import lax

HEAD_SIZE = 128
LSTEP = 128
R_DEV = 256
QUERY_FEATURES = 4096
KW = 512
RESP = 4096
PROMPT = 1024


def shared_prompt(key):
    prompt_base = jnp.clip(jax.random.normal(key, (PROMPT, KW), jnp.float32), -6.0, 6.0)
    return prompt_base


def draw_keys_prompt(key, part):
    prompt_base = shared_prompt(key)
    return prompt_base.astype(jnp.bfloat16)


def draw_queries(key, part):
    key = jax.random.fold_in(key, 3)
    query_base = jnp.clip(jax.random.normal(key, (RESP, QUERY_FEATURES), jnp.float32), -6.0, 6.0)
    return query_base.astype(jnp.bfloat16)


def draw_resp_len(key, part):
    key = jax.random.fold_in(key, 9)
    rollout_batch = RESP // R_DEV
    granules = R_DEV // LSTEP
    counts = jax.random.randint(key, (rollout_batch,), 1, granules + 1)
    longest = jax.random.randint(jax.random.fold_in(key, 1), (), 0, rollout_batch)
    counts = counts.at[longest].set(granules)
    return (counts * LSTEP).astype(jnp.int32)


def level_of(own_key, dims, cuts, low, high):
    gain, own = 1.0, jax.random.fold_in(own_key, 6)
    for position, shards_of in cuts:
        heights = jnp.exp(jax.random.uniform(jax.random.fold_in(own, position), (shards_of,), jnp.float32, low / len(cuts), high / len(cuts)))
        gain = gain * jnp.repeat(heights, dims[position] // shards_of).reshape([-1 if axis == position else 1 for axis in range(len(dims))])
    return gain


def normal_values(key, extent, deviation, reach, shards=(), kind=jnp.bfloat16):
    loudness = level_of(key, extent, shards, -0.22, 0.18) if shards else 1.0
    drawn = jax.random.normal(key, extent, jnp.float32) * deviation * loudness
    return jnp.minimum(jnp.maximum(drawn, -reach), reach).astype(kind)


def setup_inputs(seed: int = 0, part: int = 0) -> dict:
    keys = jax.random.split(jax.random.key(seed), 8)
    own_keys = jax.random.split(jax.random.fold_in(keys[7], part), 8)
    return {
        "queries": draw_queries(jax.random.fold_in(jax.random.fold_in(keys[7], part), 71), part),
        "keys_resp": normal_values(own_keys[1], (RESP, KW), 1.0, 6.0, ((0, 16),)),
        "values_resp": normal_values(own_keys[2], (RESP, KW), 2.0, 12.0, ((0, 16),)),
        "keys_prompt": draw_keys_prompt(jax.random.fold_in(jax.random.fold_in(keys[7], part), 71), part),
        "values_prompt": normal_values(own_keys[4], (PROMPT, KW), 2.0, 12.0, ((0, 16),)),
        "grad_out": normal_values(own_keys[5], (RESP, QUERY_FEATURES), 8.0, 48.0, ((0, 16),)),
        "resp_len": draw_resp_len(jax.random.fold_in(jax.random.fold_in(keys[7], part), 71), part),
    }


def rollout_grads(query_rows, key_rows, value_rows, grad_rows, length, keys_prompt, values_prompt):
    prompt_n = keys_prompt.shape[0]
    resp_rows = query_rows.shape[0]
    all_keys = jnp.concatenate([keys_prompt, key_rows], 0).astype(jnp.float32)
    all_values = jnp.concatenate([values_prompt, value_rows], 0).astype(jnp.float32)
    key_span = all_keys.shape[0]
    heads_kv = all_keys.shape[1] // HEAD_SIZE
    groups = query_rows.shape[1] // all_keys.shape[1]
    query_pos = jnp.arange(resp_rows, dtype=jnp.int32)
    is_live = query_pos < length
    masked = jnp.where(is_live[:, None], grad_rows, jnp.zeros_like(grad_rows))
    query_four = query_rows.astype(jnp.float32).reshape(resp_rows, heads_kv, groups, HEAD_SIZE)
    grad_four = masked.astype(jnp.float32).reshape(resp_rows, heads_kv, groups, HEAD_SIZE)
    key_three = all_keys.reshape(key_span, heads_kv, HEAD_SIZE)
    value_three = all_values.reshape(key_span, heads_kv, HEAD_SIZE)
    att_scale = HEAD_SIZE ** -0.5
    scores = jnp.einsum('rhgd,lhd->hgrl', query_four, key_three) * att_scale
    key_pos = jnp.arange(key_span, dtype=jnp.int32)
    visible = (key_pos[None, :] < prompt_n) | (key_pos[None, :] - prompt_n <= query_pos[:, None])
    scores = jnp.where(visible[None, None], scores, -jnp.inf)
    row_max = jnp.max(scores, axis=-1)
    log_total = row_max + jnp.log(jnp.sum(jnp.exp(scores - row_max[..., None]), axis=-1))
    probs = jnp.exp(scores - log_total[..., None])
    grad_probs = jnp.einsum('rhgd,lhd->hgrl', grad_four, value_three)
    deltas = jnp.sum(probs * grad_probs, axis=-1)
    grad_scores = probs * (grad_probs - deltas[..., None])
    probs_low = lax.optimization_barrier(probs.astype(jnp.bfloat16)).astype(jnp.float32)
    scores_low = lax.optimization_barrier(grad_scores.astype(jnp.bfloat16)).astype(jnp.float32)
    grad_query = (jnp.einsum('hgrl,lhd->rhgd', scores_low, key_three) * att_scale).reshape(resp_rows, -1)
    key_sums = jnp.einsum('hgrl,rhgd->lhd', scores_low, query_four).reshape(key_span, -1) * att_scale
    value_sums = jnp.einsum('hgrl,rhgd->lhd', probs_low, grad_four).reshape(key_span, -1)
    return grad_query.astype(jnp.bfloat16), key_sums, value_sums


def reference(queries, keys_resp, values_resp, keys_prompt, values_prompt, grad_out, resp_len):
    prompt_n = keys_prompt.shape[0]
    rollout_batch = queries.shape[0] // R_DEV
    query_set = queries.reshape(rollout_batch, R_DEV, -1)
    key_set = keys_resp.reshape(rollout_batch, R_DEV, -1)
    value_set = values_resp.reshape(rollout_batch, R_DEV, -1)
    grad_set = grad_out.reshape(rollout_batch, R_DEV, -1)

    def one_rollout(inputs):
        return rollout_grads(inputs[0], inputs[1], inputs[2], inputs[3], inputs[4], keys_prompt, values_prompt)

    grad_query, key_sums, value_sums = lax.map(one_rollout, (query_set, key_set, value_set, grad_set, resp_len))
    grad_queries = grad_query.reshape(queries.shape[0], -1)
    grad_keys_resp = key_sums[:, prompt_n:].reshape(queries.shape[0], -1).astype(jnp.bfloat16)
    grad_values_resp = value_sums[:, prompt_n:].reshape(queries.shape[0], -1).astype(jnp.bfloat16)
    key_terms_low = lax.optimization_barrier(key_sums[:, :prompt_n].astype(jnp.bfloat16)).astype(jnp.float32)
    value_terms_low = lax.optimization_barrier(value_sums[:, :prompt_n].astype(jnp.bfloat16)).astype(jnp.float32)
    grad_keys_prompt = jnp.sum(key_terms_low, axis=0).astype(jnp.bfloat16)
    grad_values_prompt = jnp.sum(value_terms_low, axis=0).astype(jnp.bfloat16)
    return grad_queries, grad_keys_resp, grad_values_resp, grad_keys_prompt, grad_values_prompt
```

```python
import functools

import jax
import jax.numpy as jnp
from jax import lax
from jax.experimental import pallas as pl
from jax.experimental.pallas import tpu as pltpu
from jax.sharding import PartitionSpec as P

D = 128
HK = 4
G = 8
ROWS = 256
PROMPT = 1024
SPAN = PROMPT + ROWS
SHARD = 64
CHIPS = 8
HALF = CHIPS * SHARD
PAIRS = HK * G // 2
BLK = 256
W = 2 * ROWS
SCALE = D**-0.5
LOG2E = 1.4426950408889634
NEG = -1e30
BF = jnp.bfloat16
F32 = jnp.float32


def dot(a, b):
    return lax.dot_general(a, b, (((1,), (0,)), ((), ())), preferred_element_type=F32)


def fold(x, op):
    return op(x.reshape(x.shape[0] // 8, 8, x.shape[1]), axis=0)


def lanes(i, n=1):
    return pl.ds(pl.multiple_of(i * D, D), n * D)


def kernel(
    q_hbm, g_hbm, kr_hbm, vr_hbm, kp_hbm, vp_hbm, len_ref,
    dq_hbm, dkr_hbm, dvr_hbm, dkp_hbm, dvp_hbm,
    q_in, g_in, kv, s0, s1, d0, d1, p0, p1, mx, lx, dx, ms, ds_, rs, q_t, g_t, k_t, gs, qs,
    dq_acc, bias, acc, dq_out, part, sib, comb, land, fin_out,
    in_sem, own_sem, dq_sem, fin_sem, ag_send, ag_recv, rl_send, rl_recv, sx_send, sx_recv, sc_send, sc_recv,
):
    s_buf, d_buf, p_buf = [s0, s1], [d0, d1], [p0, p1]
    me = lax.axis_index("seq")
    core, chip = lax.rem(me, 2), me // 2
    sibling = me + 1 - 2 * core

    def peer(o):
        return 2 * lax.rem(chip + o, CHIPS) + core

    def remote(src, dst, send, recv, to):
        return pltpu.make_async_remote_copy(
            src_ref=src, dst_ref=dst, send_sem=send, recv_sem=recv,
            device_id={"seq": to}, device_id_type=pl.DeviceIdType.MESH,
        )

    own = pl.ds(pl.multiple_of(core * HALF + chip * SHARD, SHARD), SHARD)
    mine = pl.ds(pl.multiple_of(core * HALF, HALF), HALF)
    theirs = pl.ds(pl.multiple_of((1 - core) * HALF, HALF), HALF)

    own_copies = []
    for h in range(HK):
        for w, (p_hbm, r_hbm) in enumerate(((kp_hbm, kr_hbm), (vp_hbm, vr_hbm))):
            col = pl.ds(h * D, D)
            c = pltpu.make_async_copy(p_hbm.at[:, col], kv.at[h, w, own, :], own_sem.at[h, w, 0])
            c.start()
            r = pltpu.make_async_copy(r_hbm.at[:, col], kv.at[h, w, pl.ds(PROMPT, ROWS), :], own_sem.at[h, w, 1])
            r.start()
            own_copies.append((c, r))
    q_copy = pltpu.make_async_copy(q_hbm, q_in, in_sem.at[0])
    g_copy = pltpu.make_async_copy(g_hbm, g_in, in_sem.at[1])
    q_copy.start()
    g_copy.start()

    barrier = pltpu.get_barrier_semaphore()
    for o in range(1, CHIPS):
        pl.semaphore_signal(barrier, inc=1, device_id={"seq": peer(o)}, device_id_type=pl.DeviceIdType.MESH)
    pl.semaphore_signal(barrier, inc=1, device_id={"seq": sibling}, device_id_type=pl.DeviceIdType.MESH)
    pl.semaphore_wait(barrier, CHIPS)

    for h in range(HK):
        own_copies[2 * h][0].wait()
        own_copies[2 * h + 1][0].wait()
        blk = kv.at[h, :, own, :]
        for o in range(1, CHIPS):
            remote(blk, blk, ag_send.at[h], ag_recv.at[h], peer(o)).start()

    def seven(h):
        return kv.at[h, :, pl.ds(0, (CHIPS - 1) * SHARD), :]

    def relay(h):
        x = seven(h)
        pltpu.make_async_copy(x, x, ag_recv.at[h]).wait()
        y = kv.at[h, :, mine, :]
        remote(y, y, rl_send.at[h], rl_recv.at[h], sibling).start()

    def relayed(h):
        y = kv.at[h, :, theirs, :]
        remote(y, y, rl_send.at[h], rl_recv.at[h], sibling).wait_recv()

    def keys_ready(h):
        relayed(h)
        k_t[h] = kv[h, 0].T

    q_copy.wait()
    g_copy.wait()
    live = lax.broadcasted_iota(jnp.int32, (D, ROWS), 1) < len_ref[0]

    def prep(i, _):
        q_t[i] = q_in[:, lanes(i)].T
        gt = g_in[:, lanes(i)].T.astype(F32)
        g_t[i] = jnp.where(live, gt, 0.0).astype(BF)
        return 0

    lax.fori_loop(0, HK * G, prep, 0)
    acc[...] = jnp.zeros(acc.shape, F32)
    key = lax.broadcasted_iota(jnp.int32, (BLK, ROWS), 0)
    row = lax.broadcasted_iota(jnp.int32, (BLK, ROWS), 1)
    bias[...] = jnp.where(key <= row, 0.0, NEG).astype(F32)
    mx[...] = jnp.full(mx.shape, NEG, F32)
    lx[...] = jnp.zeros(lx.shape, F32)
    dx[...] = jnp.zeros(dx.shape, F32)
    for c, r in own_copies:
        r.wait()

    def stage_a(t, par, c):
        h, rows = t // 4, pl.ds(c * BLK, BLK)
        for u in range(2):
            ls = slice(u * ROWS, (u + 1) * ROWS)
            s = dot(kv[h, 0, rows, :], q_t[t * 2 + u])
            if c * BLK >= PROMPT:
                s = s + bias[...]
            s_buf[par][rows, ls] = s
            mx[par, :, ls] = jnp.maximum(mx[par, :, ls], fold(s, jnp.max))

    def stage_b(t, par, c):
        h, rows = t // 4, pl.ds(c * BLK, BLK)
        for u in range(2):
            ls = slice(u * ROWS, (u + 1) * ROWS)
            p = jnp.exp2(s_buf[par][rows, ls] * F32(SCALE * LOG2E) - ms[par, 0:1, ls])
            lx[par, :, ls] += fold(p, jnp.sum)
            p_buf[par][rows, ls] = p.astype(BF)
            d = dot(kv[h, 1, rows, :], g_t[t * 2 + u])
            d_buf[par][rows, ls] = d
            dx[par, :, ls] += fold(p * d, jnp.sum)

    def stage_c(t, par, c):
        h, rows = t // 4, pl.ds(c * BLK, BLK)
        p = p_buf[par][rows, :]
        ds = p * (d_buf[par][rows, :] - ds_[par, 0:1, :]).astype(BF)
        acc[1, :, rows] += dot(gs[par], p.T)
        acc[0, :, rows] += dot(qs[par], ds.T)
        dq_acc[...] += dot(k_t[h, :, rows], ds)

    def max_done(par):
        m = jnp.max(mx[par], axis=0, keepdims=True) * F32(SCALE * LOG2E)
        ms[par] = jnp.broadcast_to(m, (8, W))
        mx[par] = jnp.full((8, W), NEG, F32)

    def sums_done(t, par):
        r = 1.0 / jnp.sum(lx[par], axis=0, keepdims=True)
        ds_[par] = jnp.broadcast_to(jnp.sum(dx[par], axis=0, keepdims=True) * r, (8, W))
        rs[par] = jnp.broadcast_to(r, (8, W))
        lx[par] = jnp.zeros((8, W), F32)
        dx[par] = jnp.zeros((8, W), F32)
        for u in range(2):
            ls = slice(u * ROWS, (u + 1) * ROWS)
            gs[par, :, ls] = (g_t[t * 2 + u].astype(F32) * r[:, ls]).astype(BF)
            qs[par, :, ls] = (q_t[t * 2 + u].astype(F32) * r[:, ls]).astype(BF)

    def dq_copy(t, par):
        return pltpu.make_async_copy(dq_out.at[par], dq_hbm.at[:, lanes(2 * t, 2)], dq_sem.at[par])

    def dq_done(t, par):
        for u in range(2):
            ls = slice(u * ROWS, (u + 1) * ROWS)
            x = dq_acc[:, ls] * (rs[par, 0:1, ls] * F32(SCALE))
            dq_out[par, :, u * D : (u + 1) * D] = x.astype(BF).T
        dq_copy(t, par).start()

    def step(t, par, a=True, b=True, c=True, wait_dq=True):
        if c:
            dq_acc[...] = jnp.zeros((D, W), F32)
            sums_done(t - 2, par)
        if b:
            max_done(1 - par)
        for k in range(SPAN // BLK):
            if a:
                stage_a(t, par, k)
            if b:
                stage_b(t - 1, 1 - par, k)
            if c:
                stage_c(t - 2, par, k)
        if c:
            if wait_dq is True:
                dq_copy(t - 4, par).wait()
            elif wait_dq is not False:

                @pl.when(wait_dq)
                def _():
                    dq_copy(t - 4, par).wait()

            dq_done(t - 2, par)

    def resp_copy(h, w):
        out = (dkr_hbm, dvr_hbm)[w]
        return pltpu.make_async_copy(part.at[h, w, pl.ds(PROMPT, ROWS), :], out.at[:, lanes(h)], fin_sem.at[h, w])

    def sum_copy(h, w):
        out = (dkp_hbm, dvp_hbm)[w]
        return pltpu.make_async_copy(fin_out.at[h, w], out.at[:, lanes(h)], fin_sem.at[h, 2 + w])

    def swap(h):
        return remote(part.at[h, :, theirs, :], sib.at[h], sx_send.at[h], sx_recv.at[h], sibling)

    def scatter_1(h):
        part[h, 0] = (acc[0] * F32(SCALE)).astype(BF).T
        part[h, 1] = acc[1].astype(BF).T
        acc[...] = jnp.zeros(acc.shape, F32)
        swap(h).start()
        for w in range(2):
            resp_copy(h, w).start()

    def scatter_2(h):
        swap(h).wait_recv()
        for w in range(2):
            comb[h, w] = (part[h, w, mine, :].astype(F32) + sib[h, w].astype(F32)).astype(BF)
        for o in range(1, CHIPS):
            to = lax.rem(chip + o, CHIPS)
            rows = pl.ds(pl.multiple_of(to * SHARD, SHARD), SHARD)
            remote(comb.at[h, :, rows, :], land.at[h, CHIPS - 1 - o], sc_send.at[h], sc_recv.at[h], peer(o)).start()

    def scatter_3(h):
        x = land.at[h]
        pltpu.make_async_copy(x, x, sc_recv.at[h]).wait()
        rows = pl.ds(pl.multiple_of(chip * SHARD, SHARD), SHARD)
        for w in range(2):
            total = comb[h, w, rows, :].astype(F32)
            for o in range(CHIPS - 1):
                total = total + land[h, o, w].astype(F32)
            fin_out[h, w] = total.astype(BF)
            sum_copy(h, w).start()

    relay(0)
    keys_ready(0)
    step(0, 0, b=False, c=False)
    step(1, 1, c=False)

    def four(z, _):
        t = 4 * z + 2
        relay(z + 1)

        @pl.when(z > 0)
        def _():
            scatter_1(z - 1)

        @pl.when(z > 1)
        def _():
            scatter_3(z - 2)

        step(t, 0, wait_dq=z > 0)
        step(t + 1, 1, wait_dq=z > 0)
        keys_ready(z + 1)

        @pl.when(z > 0)
        def _():
            scatter_2(z - 1)

        step(t + 2, 0)
        step(t + 3, 1)
        return 0

    lax.fori_loop(0, HK - 1, four, 0)
    scatter_1(HK - 2)
    scatter_3(HK - 3)
    step(14, 0)
    step(15, 1)
    scatter_2(HK - 2)
    step(16, 0, a=False)
    step(17, 1, a=False, b=False)
    scatter_1(HK - 1)
    scatter_3(HK - 2)
    scatter_2(HK - 1)
    scatter_3(HK - 1)

    dq_copy(PAIRS - 2, 0).wait()
    dq_copy(PAIRS - 1, 1).wait()
    for h in range(HK):
        x = seven(h)
        pltpu.make_async_copy(x, x, ag_send.at[h]).wait()
        y = kv.at[h, :, mine, :]
        remote(y, y, rl_send.at[h], rl_recv.at[h], sibling).wait_send()
        swap(h).wait_send()
        x = land.at[h]
        pltpu.make_async_copy(x, x, sc_send.at[h]).wait()
        for w in range(2):
            resp_copy(h, w).wait()
            sum_copy(h, w).wait()


def shards(queries, keys_resp, values_resp, keys_prompt, values_prompt, grad_out, resp_len):
    vm = pltpu.VMEM
    dma = pltpu.SemaphoreType.DMA
    wide = HK * D
    hbm = pl.BlockSpec(memory_space=pl.ANY)
    return pl.pallas_call(
        kernel,
        out_shape=(
            jax.ShapeDtypeStruct((ROWS, HK * G * D), BF),
            jax.ShapeDtypeStruct((ROWS, wide), BF),
            jax.ShapeDtypeStruct((ROWS, wide), BF),
            jax.ShapeDtypeStruct((SHARD, wide), BF),
            jax.ShapeDtypeStruct((SHARD, wide), BF),
        ),
        in_specs=[hbm] * 6 + [pl.BlockSpec(memory_space=pltpu.SMEM)],
        out_specs=(hbm,) * 5,
        scratch_shapes=[
            vm((ROWS, HK * G * D), BF),
            vm((ROWS, HK * G * D), BF),
            vm((HK, 2, SPAN, D), BF),
            vm((SPAN, W), F32), vm((SPAN, W), F32),
            vm((SPAN, W), F32), vm((SPAN, W), F32),
            vm((SPAN, W), BF), vm((SPAN, W), BF),
            vm((2, 8, W), F32), vm((2, 8, W), F32), vm((2, 8, W), F32),
            vm((2, 8, W), F32), vm((2, 8, W), F32), vm((2, 8, W), F32),
            vm((HK * G, D, ROWS), BF), vm((HK * G, D, ROWS), BF),
            vm((HK, D, SPAN), BF),
            vm((2, D, W), BF), vm((2, D, W), BF),
            vm((D, W), F32),
            vm((BLK, ROWS), F32),
            vm((2, D, SPAN), F32),
            vm((2, ROWS, 2 * D), BF),
            vm((HK, 2, SPAN, D), BF),
            vm((HK, 2, HALF, D), BF),
            vm((HK, 2, HALF, D), BF),
            vm((HK, CHIPS - 1, 2, SHARD, D), BF),
            vm((HK, 2, SHARD, D), BF),
            dma((2,)), dma((HK, 2, 2)), dma((2,)), dma((HK, 4)),
            dma((HK,)), dma((HK,)), dma((HK,)), dma((HK,)), dma((HK,)), dma((HK,)), dma((HK,)), dma((HK,)),
        ],
        compiler_params=pltpu.CompilerParams(
            collective_id=0, has_side_effects=True, vmem_limit_bytes=56 * 2**20
        ),
    )(queries, grad_out, keys_resp, values_resp, keys_prompt, values_prompt, resp_len)


def solution(mesh):
    rows = P(("grp", "seq"), None)
    return jax.shard_map(
        shards,
        mesh=mesh,
        in_specs=(rows,) * 6 + (P(("grp", "seq")),),
        out_specs=(rows,) * 5,
        check_vma=False,
    )
```

```python
import functools

import jax
import jax.numpy as jnp
from jax import lax
from jax.experimental import pallas as pl
from jax.experimental.pallas import tpu as pltpu
from jax.sharding import PartitionSpec as P

D = 128
HK = 4
G = 8
ROWS = 256
PROMPT = 1024
SPAN = PROMPT + ROWS
SHARD = 64
CHIPS = 8
HALF = CHIPS * SHARD
PAIRS = HK * G // 2
BLK = 256
W = 2 * ROWS
SCALE = D**-0.5
LOG2E = 1.4426950408889634
NEG = -1e30
BF = jnp.bfloat16
F32 = jnp.float32


def dot(a, b):
    return lax.dot_general(a, b, (((1,), (0,)), ((), ())), preferred_element_type=F32)


def fold(x, op):
    return op(x.reshape(x.shape[0] // 8, 8, x.shape[1]), axis=0)


def lanes(i, n=1):
    return pl.ds(pl.multiple_of(i * D, D), n * D)


def kernel(
    q_hbm, g_hbm, kr_hbm, vr_hbm, kp_hbm, vp_hbm, len_ref,
    dq_ref, dkr_ref, dvr_ref, dkp_ref, dvp_ref,
    kv, s0, s1, d0, d1, p0, p1, dsb, mx, lx, dx, ms, ds_, rs, q_t, g_t, k_t, gs, qs,
    bias, acc, part, sib, comb, land,
    in_sem, own_sem, ag_send, ag_recv, rl_send, rl_recv, sx_send, sx_recv, sc_send, sc_recv,
):
    s_buf, d_buf, p_buf = [s0, s1], [d0, d1], [p0, p1]
    me = lax.axis_index("seq")
    core, chip = lax.rem(me, 2), me // 2
    sibling = me + 1 - 2 * core

    def peer(o):
        return 2 * lax.rem(chip + o, CHIPS) + core

    def remote(src, dst, send, recv, to):
        return pltpu.make_async_remote_copy(
            src_ref=src, dst_ref=dst, send_sem=send, recv_sem=recv,
            device_id={"seq": to}, device_id_type=pl.DeviceIdType.MESH,
        )

    own = pl.ds(pl.multiple_of(core * HALF + chip * SHARD, SHARD), SHARD)
    mine = pl.ds(pl.multiple_of(core * HALF, HALF), HALF)
    theirs = pl.ds(pl.multiple_of((1 - core) * HALF, HALF), HALF)

    own_copies = []
    for h in range(HK):
        for w, (p_hbm, r_hbm) in enumerate(((kp_hbm, kr_hbm), (vp_hbm, vr_hbm))):
            col = pl.ds(h * D, D)
            c = pltpu.make_async_copy(p_hbm.at[:, col], kv.at[h, w, own, :], own_sem.at[h, w, 0])
            c.start()
            r = pltpu.make_async_copy(r_hbm.at[:, col], kv.at[h, w, pl.ds(PROMPT, ROWS), :], own_sem.at[h, w, 1])
            r.start()
            own_copies.append((c, r))
    q_copy = pltpu.make_async_copy(q_hbm, dq_ref, in_sem.at[0])
    q_copy.start()
    g_copies = []
    for j in range(HK * G * D // W):
        to = dsb.at[PAIRS - 2 + j // 4, pl.ds(j % 4 * ROWS, ROWS), :]
        g_copies.append(pltpu.make_async_copy(g_hbm.at[:, pl.ds(j * W, W)], to, in_sem.at[1 + j]))
        g_copies[-1].start()

    barrier = pltpu.get_barrier_semaphore()
    for o in range(1, CHIPS):
        pl.semaphore_signal(barrier, inc=1, device_id={"seq": peer(o)}, device_id_type=pl.DeviceIdType.MESH)
    pl.semaphore_signal(barrier, inc=1, device_id={"seq": sibling}, device_id_type=pl.DeviceIdType.MESH)
    pl.semaphore_wait(barrier, CHIPS)

    def sends(h, w):
        blk = kv.at[h, w, own, :]
        for o in range(1, CHIPS):
            remote(blk, blk, ag_send.at[h, w], ag_recv.at[h, w], peer(o)).start()

    def seven(h, w):
        return kv.at[h, w, pl.ds(0, (CHIPS - 1) * SHARD), :]

    def relay(h, w):
        x = seven(h, w)
        pltpu.make_async_copy(x, x, ag_recv.at[h, w]).wait()
        y = kv.at[h, w, mine, :]
        remote(y, y, rl_send.at[h, w], rl_recv.at[h, w], sibling).start()

    def relayed(h, w):
        y = kv.at[h, w, theirs, :]
        remote(y, y, rl_send.at[h, w], rl_recv.at[h, w], sibling).wait_recv()

    own_copies[0][0].wait()
    sends(0, 0)
    own_copies[1][0].wait()
    sends(0, 1)
    for c, _ in own_copies[2:]:
        c.wait()

    q_copy.wait()
    for c in g_copies:
        c.wait()
    live = lax.broadcasted_iota(jnp.int32, (D, ROWS), 1) < len_ref[0]

    def prep(i, _):
        q_t[i] = dq_ref[:, lanes(i)].T
        from_row = pl.ds(pl.multiple_of(i // 4 % 4 * ROWS, ROWS), ROWS)
        gt = dsb[PAIRS - 2 + i // 16, from_row, lanes(i % 4)].T.astype(F32)
        g_t[i] = jnp.where(live, gt, 0.0).astype(BF)
        return 0

    def prep_four(i, _):
        for u in range(4):
            prep(4 * i + u, 0)
        return 0

    prep(0, 0)
    prep(1, 0)
    acc[...] = jnp.zeros(acc.shape, F32)
    key = lax.broadcasted_iota(jnp.int32, (BLK, ROWS), 0)
    row = lax.broadcasted_iota(jnp.int32, (BLK, ROWS), 1)
    bias[...] = jnp.where(key <= row, 0.0, NEG).astype(F32)
    mx[...] = jnp.full(mx.shape, NEG, F32)
    lx[...] = jnp.zeros(lx.shape, F32)
    dx[...] = jnp.zeros(dx.shape, F32)
    for c, r in own_copies:
        r.wait()

    def stage_a(t, par, c):
        h, rows = t // 4, pl.ds(c * BLK, BLK)
        for u in range(2):
            ls = slice(u * ROWS, (u + 1) * ROWS)
            s = dot(kv[h, 0, rows, :], q_t[t * 2 + u])
            if c * BLK >= PROMPT:
                s = s + bias[...]
            s_buf[par][rows, ls] = s
            mx[par, :, ls] = jnp.maximum(mx[par, :, ls], fold(s, jnp.max))

    def stage_b(t, par, c):
        h, rows = t // 4, pl.ds(c * BLK, BLK)
        for u in range(2):
            ls = slice(u * ROWS, (u + 1) * ROWS)
            p = jnp.exp2(s_buf[par][rows, ls] * F32(SCALE * LOG2E) - ms[par, 0:1, ls])
            lx[par, :, ls] += fold(p, jnp.sum)
            p_buf[par][rows, ls] = p.astype(BF)
            d = dot(kv[h, 1, rows, :], g_t[t * 2 + u])
            d_buf[par][rows, ls] = d
            dx[par, :, ls] += fold(p * d, jnp.sum)

    def stage_c(t, par, c):
        rows = pl.ds(c * BLK, BLK)
        p = p_buf[par][rows, :]
        ds = p * (d_buf[par][rows, :] - ds_[par, 0:1, :]).astype(BF)
        dsb[t, rows, :] = ds
        acc[1, :, rows] += dot(gs[par], p.T)
        acc[0, :, rows] += dot(qs[par], ds.T)

    def max_done(par):
        m = jnp.max(mx[par], axis=0, keepdims=True) * F32(SCALE * LOG2E)
        ms[par] = jnp.broadcast_to(m, (8, W))
        mx[par] = jnp.full((8, W), NEG, F32)

    def sums_done(t, par):
        r = 1.0 / jnp.sum(lx[par], axis=0, keepdims=True)
        ds_[par] = jnp.broadcast_to(jnp.sum(dx[par], axis=0, keepdims=True) * r, (8, W))
        rs[t] = jnp.broadcast_to(r * F32(SCALE), (8, W))
        lx[par] = jnp.zeros((8, W), F32)
        dx[par] = jnp.zeros((8, W), F32)
        for u in range(2):
            ls = slice(u * ROWS, (u + 1) * ROWS)
            gs[par, :, ls] = (g_t[t * 2 + u].astype(F32) * r[:, ls]).astype(BF)
            qs[par, :, ls] = (q_t[t * 2 + u].astype(F32) * r[:, ls]).astype(BF)

    def grad_queries(h):
        k_t[...] = kv[h, 0].T
        for j in range(PAIRS // HK):
            t = h * (PAIRS // HK) + j
            x = dot(k_t[...], dsb[t]) * rs[t, 0:1, :]
            for u in range(2):
                dq_ref[:, lanes(2 * t + u)] = x[:, u * ROWS : (u + 1) * ROWS].astype(BF).T

    def step(t, par, a=True, b=True, c=True):
        if c:
            sums_done(t - 2, par)
        if b:
            max_done(1 - par)
        for k in range(SPAN // BLK):
            if a:
                stage_a(t, par, k)
            if b:
                stage_b(t - 1, 1 - par, k)
            if c:
                stage_c(t - 2, par, k)

    def swap(h):
        return remote(part.at[h, :, theirs, :], sib.at[h], sx_send.at[h], sx_recv.at[h], sibling)

    def scatter_1(h):
        part[h, 0] = (acc[0] * F32(SCALE)).astype(BF).T
        part[h, 1] = acc[1].astype(BF).T
        acc[...] = jnp.zeros(acc.shape, F32)
        swap(h).start()
        dkr_ref[:, lanes(h)] = part[h, 0, PROMPT:, :]
        dvr_ref[:, lanes(h)] = part[h, 1, PROMPT:, :]

    def scatter_2(h):
        swap(h).wait_recv()
        for w in range(2):
            comb[h, w] = (part[h, w, mine, :].astype(F32) + sib[h, w].astype(F32)).astype(BF)
        for o in range(1, CHIPS):
            to = lax.rem(chip + o, CHIPS)
            rows = pl.ds(pl.multiple_of(to * SHARD, SHARD), SHARD)
            remote(comb.at[h, :, rows, :], land.at[h, CHIPS - 1 - o], sc_send.at[h], sc_recv.at[h], peer(o)).start()

    def scatter_3(h):
        x = land.at[h]
        pltpu.make_async_copy(x, x, sc_recv.at[h]).wait()
        rows = pl.ds(pl.multiple_of(chip * SHARD, SHARD), SHARD)
        for w, out in enumerate((dkp_ref, dvp_ref)):
            total = comb[h, w, rows, :].astype(F32)
            for o in range(CHIPS - 1):
                total = total + land[h, o, w].astype(F32)
            out[:, lanes(h)] = total.astype(BF)

    relay(0, 0)
    sends(1, 0)
    sends(1, 1)
    lax.fori_loop(0, HK * G // 4, prep_four, 0)
    relayed(0, 0)
    step(0, 0, b=False, c=False)
    relay(0, 1)
    relayed(0, 1)
    step(1, 1, c=False)

    def four(z, _):
        t = 4 * z + 2
        relay(z + 1, 0)
        relay(z + 1, 1)

        @pl.when(z < HK - 2)
        def _():
            sends(z + 2, 0)
            sends(z + 2, 1)

        @pl.when(z > 0)
        def _():
            scatter_1(z - 1)

        step(t, 0)
        step(t + 1, 1)
        relayed(z + 1, 0)
        relayed(z + 1, 1)

        @pl.when(z > 0)
        def _():
            scatter_2(z - 1)

        @pl.when(z > 1)
        def _():
            scatter_3(z - 2)

        step(t + 2, 0)
        step(t + 3, 1)
        return 0

    lax.fori_loop(0, HK - 1, four, 0)
    scatter_1(HK - 2)
    step(14, 0)
    step(15, 1)
    scatter_2(HK - 2)
    scatter_3(HK - 3)
    step(16, 0, a=False)
    step(17, 1, a=False, b=False)
    scatter_1(HK - 1)
    grad_queries(0)
    scatter_2(HK - 1)
    grad_queries(1)
    scatter_3(HK - 2)
    grad_queries(2)
    grad_queries(3)
    scatter_3(HK - 1)

    for h in range(HK):
        for w in range(2):
            x = seven(h, w)
            pltpu.make_async_copy(x, x, ag_send.at[h, w]).wait()
            y = kv.at[h, w, mine, :]
            remote(y, y, rl_send.at[h, w], rl_recv.at[h, w], sibling).wait_send()
        swap(h).wait_send()
        x = land.at[h]
        pltpu.make_async_copy(x, x, sc_send.at[h]).wait()


def publish(*refs):
    n = len(refs) // 2
    copies = [pltpu.make_async_copy(refs[i], refs[n + i], refs[-1].at[i]) for i in range(n)]
    for c in copies:
        c.start()
    for c in copies:
        c.wait()


def shards(queries, keys_resp, values_resp, keys_prompt, values_prompt, grad_out, resp_len):
    vm = pltpu.VMEM
    dma = pltpu.SemaphoreType.DMA
    wide = HK * D
    hbm = pl.BlockSpec(memory_space=pl.ANY)
    outs = pl.pallas_call(
        kernel,
        out_shape=(
            vm((ROWS, HK * G * D), BF),
            vm((ROWS, wide), BF),
            vm((ROWS, wide), BF),
            vm((SHARD, wide), BF),
            vm((SHARD, wide), BF),
        ),
        in_specs=[hbm] * 6 + [pl.BlockSpec(memory_space=pltpu.SMEM)],
        out_specs=(pl.BlockSpec(memory_space=vm),) * 5,
        scratch_shapes=[
            vm((HK, 2, SPAN, D), BF),
            vm((SPAN, W), F32), vm((SPAN, W), F32),
            vm((SPAN, W), F32), vm((SPAN, W), F32),
            vm((SPAN, W), BF), vm((SPAN, W), BF),
            vm((PAIRS, SPAN, W), BF),
            vm((2, 8, W), F32), vm((2, 8, W), F32), vm((2, 8, W), F32),
            vm((2, 8, W), F32), vm((2, 8, W), F32), vm((PAIRS, 8, W), F32),
            vm((HK * G, D, ROWS), BF), vm((HK * G, D, ROWS), BF),
            vm((D, SPAN), BF),
            vm((2, D, W), BF), vm((2, D, W), BF),
            vm((BLK, ROWS), F32),
            vm((2, D, SPAN), F32),
            vm((HK, 2, SPAN, D), BF),
            vm((HK, 2, HALF, D), BF),
            vm((HK, 2, HALF, D), BF),
            vm((HK, CHIPS - 1, 2, SHARD, D), BF),
            dma((9,)), dma((HK, 2, 2)),
            dma((HK, 2)), dma((HK, 2)), dma((HK, 2)), dma((HK, 2)), dma((HK,)), dma((HK,)), dma((HK,)), dma((HK,)),
        ],
        compiler_params=pltpu.CompilerParams(
            collective_id=0, has_side_effects=True, vmem_limit_bytes=56 * 2**20
        ),
    )(queries, grad_out, keys_resp, values_resp, keys_prompt, values_prompt, resp_len)
    return pl.pallas_call(
        publish,
        out_shape=tuple(jax.ShapeDtypeStruct(o.shape, o.dtype) for o in outs),
        in_specs=[pl.BlockSpec(memory_space=vm)] * 5,
        out_specs=(hbm,) * 5,
        scratch_shapes=[dma((5,))],
    )(*[pltpu.with_memory_space_constraint(o, vm) for o in outs])


def solution(mesh):
    rows = P(("grp", "seq"), None)
    return jax.shard_map(
        shards,
        mesh=mesh,
        in_specs=(rows,) * 6 + (P(("grp", "seq")),),
        out_specs=(rows,) * 5,
        check_vma=False,
    )
```

```python
import functools

import jax
import jax.numpy as jnp
from jax import lax
from jax.experimental import pallas as pl
from jax.experimental.pallas import tpu as pltpu
from jax.sharding import PartitionSpec as P

D = 128
HK = 4
G = 8
ROWS = 256
PROMPT = 1024
SPAN = PROMPT + ROWS
SHARD = 64
CHIPS = 8
HALF = CHIPS * SHARD
PAIRS = HK * G // 2
BLK = 256
SUB = 64
W = 2 * ROWS
SCALE = D**-0.5
LOG2E = 1.4426950408889634
NEG = -1e30
BF = jnp.bfloat16
F32 = jnp.float32


def dot(a, b):
    return lax.dot_general(a, b, (((1,), (0,)), ((), ())), preferred_element_type=F32)


def fold(x, op):
    return op(x.reshape(x.shape[0] // 8, 8, x.shape[1]), axis=0)


def lanes(i, n=1):
    return pl.ds(pl.multiple_of(i * D, D), n * D)


def kernel(
    q_hbm, g_hbm, kr_hbm, vr_hbm, kp_hbm, vp_hbm, len_ref,
    dq_ref, dkr_ref, dvr_ref, dkp_ref, dvp_ref,
    kv, s0, s1, d0, d1, p0, p1, dsb, mx, lx, dx, ms, ds_, rs, q_t, g_t, k_t, gs, qs,
    p_t, bias, acc, part, sib, land,
    in_sem, own_sem, ag_send, ag_recv, rl_send, rl_recv, sx_send, sx_recv, sc_send, sc_recv,
):
    s_buf, d_buf, p_buf = [s0, s1], [d0, d1], [p0, p1]
    me = lax.axis_index("seq")
    core, chip = lax.rem(me, 2), me // 2
    sibling = me + 1 - 2 * core

    def peer(o):
        return 2 * lax.rem(chip + o, CHIPS) + core

    def remote(src, dst, send, recv, to):
        return pltpu.make_async_remote_copy(
            src_ref=src, dst_ref=dst, send_sem=send, recv_sem=recv,
            device_id={"seq": to}, device_id_type=pl.DeviceIdType.MESH,
        )

    own = pl.ds(pl.multiple_of(core * HALF + chip * SHARD, SHARD), SHARD)
    mine = pl.ds(pl.multiple_of(core * HALF, HALF), HALF)
    theirs = pl.ds(pl.multiple_of((1 - core) * HALF, HALF), HALF)

    own_copies = []
    for h in range(HK):
        for w, (p_hbm, r_hbm) in enumerate(((kp_hbm, kr_hbm), (vp_hbm, vr_hbm))):
            col = pl.ds(h * D, D)
            c = pltpu.make_async_copy(p_hbm.at[:, col], kv.at[h, w, own, :], own_sem.at[h, w, 0])
            c.start()
            r = pltpu.make_async_copy(r_hbm.at[:, col], kv.at[h, w, pl.ds(PROMPT, ROWS), :], own_sem.at[h, w, 1])
            r.start()
            own_copies.append((c, r))
    q_copy = pltpu.make_async_copy(q_hbm, dq_ref, in_sem.at[0])
    q_copy.start()
    g_copies = []
    for j in range(HK * G * D // W):
        to = dsb.at[PAIRS - 2 + j // 4, pl.ds(j % 4 * ROWS, ROWS), :]
        g_copies.append(pltpu.make_async_copy(g_hbm.at[:, pl.ds(j * W, W)], to, in_sem.at[1 + j]))
        g_copies[-1].start()

    barrier = pltpu.get_barrier_semaphore()
    for o in range(1, CHIPS):
        pl.semaphore_signal(barrier, inc=1, device_id={"seq": peer(o)}, device_id_type=pl.DeviceIdType.MESH)
    pl.semaphore_signal(barrier, inc=1, device_id={"seq": sibling}, device_id_type=pl.DeviceIdType.MESH)
    pl.semaphore_wait(barrier, CHIPS)

    def sends(h, w):
        blk = kv.at[h, w, own, :]
        for o in range(1, CHIPS):
            remote(blk, blk, ag_send.at[h, w], ag_recv.at[h, w], peer(o)).start()

    def seven(h, w):
        return kv.at[h, w, pl.ds(0, (CHIPS - 1) * SHARD), :]

    def relay(h, w):
        x = seven(h, w)
        pltpu.make_async_copy(x, x, ag_recv.at[h, w]).wait()
        y = kv.at[h, w, mine, :]
        remote(y, y, rl_send.at[h, w], rl_recv.at[h, w], sibling).start()

    def relayed(h, w):
        y = kv.at[h, w, theirs, :]
        remote(y, y, rl_send.at[h, w], rl_recv.at[h, w], sibling).wait_recv()

    own_copies[0][0].wait()
    sends(0, 0)
    own_copies[1][0].wait()
    sends(0, 1)
    for c, _ in own_copies[2:]:
        c.wait()

    q_copy.wait()
    for c in g_copies:
        c.wait()
    live = lax.broadcasted_iota(jnp.int32, (D, ROWS), 1) < len_ref[0]

    def prep(i, _):
        qt = dq_ref[:, lanes(i)].T.astype(F32) * F32(SCALE * LOG2E)
        high = qt.astype(BF)
        q_t[i, 0:D, :] = high
        q_t[i, D : 2 * D, :] = (qt - high.astype(F32)).astype(BF)
        from_row = pl.ds(pl.multiple_of(i // 4 % 4 * ROWS, ROWS), ROWS)
        gt = dsb[PAIRS - 2 + i // 16, from_row, lanes(i % 4)].T.astype(F32)
        g_t[i] = jnp.where(live, gt, 0.0).astype(BF)
        return 0

    def prep_four(i, _):
        for u in range(4):
            prep(4 * i + u, 0)
        return 0

    acc[...] = jnp.zeros(acc.shape, F32)
    key = lax.broadcasted_iota(jnp.int32, (BLK, ROWS), 0)
    row = lax.broadcasted_iota(jnp.int32, (BLK, ROWS), 1)
    bias[...] = jnp.where(key <= row, 0.0, NEG).astype(F32)
    mx[...] = jnp.full(mx.shape, NEG, F32)
    lx[...] = jnp.zeros(lx.shape, F32)
    dx[...] = jnp.zeros(dx.shape, F32)
    for c, r in own_copies:
        r.wait()

    def stage_a(t, par, c):
        h, rows = t // 4, pl.ds(c * BLK, BLK)
        for u in range(2):
            ls = slice(u * ROWS, (u + 1) * ROWS)
            k = kv[h, 0, rows, :]
            s = dot(jnp.concatenate([k, k], axis=1), q_t[t * 2 + u])
            if c * BLK >= PROMPT:
                s = s + bias[...]
            s_buf[par][rows, ls] = s
            mx[par, :, ls] = jnp.maximum(mx[par, :, ls], fold(s, jnp.max))

    def stage_b(t, par, c):
        h, rows = t // 4, pl.ds(c * BLK, BLK)
        for u in range(2):
            ls = slice(u * ROWS, (u + 1) * ROWS)
            d = dot(kv[h, 1, rows, :], g_t[t * 2 + u])
            top, l_sum, d_sum = ms[par, 0:1, ls], lx[par, :, ls], dx[par, :, ls]
            for i in range(0, BLK, SUB):
                sub = pl.ds(c * BLK + i, SUB)
                p = jnp.exp2(s_buf[par][sub, ls] - top)
                l_sum += fold(p, jnp.sum)
                p_buf[par][sub, ls] = p.astype(BF)
                d_buf[par][sub, ls] = d[i : i + SUB]
                d_sum += fold(p * d[i : i + SUB], jnp.sum)
            lx[par, :, ls] = l_sum
            dx[par, :, ls] = d_sum

    def value_terms(par, c):
        rows = pl.ds(c * BLK, BLK)
        p_t[c % 2] = p_buf[par][rows, :].T
        acc[1, :, rows] += dot(gs[par], p_t[c % 2])

    def key_terms(t, par, c):
        rows = pl.ds(c * BLK, BLK)
        for i in range(0, BLK, SUB):
            sub = pl.ds(c * BLK + i, SUB)
            for u in range(2):
                ls = slice(u * ROWS, (u + 1) * ROWS)
                ds = (d_buf[par][sub, ls] - ds_[par, 0:1, ls]).astype(BF)
                dsb[t, sub, ls] = p_buf[par][sub, ls] * ds
        return rows

    def stage_c(t, par, c):
        rows = key_terms(t, par, c)
        value_terms(par, c)
        acc[0, :, rows] += dot(qs[par], dsb[t, rows, :].T)

    def max_done(par):
        m = jnp.max(mx[par], axis=0, keepdims=True)
        ms[par] = jnp.broadcast_to(m, (8, W))
        mx[par] = jnp.full((8, W), NEG, F32)

    def sums_done(t, par):
        r = 1.0 / jnp.sum(lx[par], axis=0, keepdims=True)
        ds_[par] = jnp.broadcast_to(jnp.sum(dx[par], axis=0, keepdims=True) * r, (8, W))
        rs[t] = jnp.broadcast_to(r * F32(SCALE), (8, W))
        lx[par] = jnp.zeros((8, W), F32)
        dx[par] = jnp.zeros((8, W), F32)
        for u in range(2):
            ls = slice(u * ROWS, (u + 1) * ROWS)
            gs[par, :, ls] = (g_t[t * 2 + u].astype(F32) * r[:, ls]).astype(BF)
            q = q_t[t * 2 + u, 0:D, :].astype(F32) + q_t[t * 2 + u, D : 2 * D, :].astype(F32)
            qs[par, :, ls] = (q * r[:, ls]).astype(BF)

    def grad_queries(h):
        k_t[...] = kv[h, 0].T
        for j in range(PAIRS // HK):
            t = h * (PAIRS // HK) + j
            x = dot(k_t[...], dsb[t]) * rs[t, 0:1, :]
            for u in range(2):
                dq_ref[:, lanes(2 * t + u)] = x[:, u * ROWS : (u + 1) * ROWS].astype(BF).T

    def step(t, par, a=True, b=True, c=True):
        if c:
            sums_done(t - 2, par)
        if b:
            max_done(1 - par)
        for k in range(SPAN // BLK):
            if a:
                stage_a(t, par, k)
            if b:
                stage_b(t - 1, 1 - par, k)
            if c:
                stage_c(t - 2, par, k)

    def swap(h, w):
        return remote(part.at[h, w, theirs, :], sib.at[h, w], sx_send.at[h, w], sx_recv.at[h, w], sibling)

    def scatter_1(h, w):
        x = acc[w] * F32(1 / LOG2E) if w == 0 else acc[w]
        part[h, w] = x.astype(BF).T
        acc[w] = jnp.zeros(acc.shape[1:], F32)
        swap(h, w).start()
        out = (dkr_ref, dvr_ref)[w]
        out[:, lanes(h)] = part[h, w, PROMPT:, :]

    def scatter_2(h, w):
        swap(h, w).wait_recv()
        part[h, w, mine, :] = (part[h, w, mine, :].astype(F32) + sib[h, w].astype(F32)).astype(BF)
        for o in range(1, CHIPS):
            to = lax.rem(chip + o, CHIPS)
            rows = pl.ds(pl.multiple_of(core * HALF + to * SHARD, SHARD), SHARD)
            remote(
                part.at[h, w, rows, :], land.at[h, w, CHIPS - 1 - o], sc_send.at[h, w], sc_recv.at[h, w], peer(o)
            ).start()

    def scatter_3(h, w):
        x = land.at[h, w]
        pltpu.make_async_copy(x, x, sc_recv.at[h, w]).wait()
        total = part[h, w, own, :].astype(F32)
        for o in range(CHIPS - 1):
            total = total + land[h, w, o].astype(F32)
        out = (dkp_ref, dvp_ref)[w]
        out[:, lanes(h)] = total.astype(BF)

    def both(f, h):
        f(h, 1)
        f(h, 0)

    half = HK * G // 8
    lax.fori_loop(0, half, prep_four, 0)
    relay(0, 0)
    sends(1, 0)
    sends(1, 1)
    lax.fori_loop(half, 2 * half, prep_four, 0)
    relay(0, 1)
    relayed(0, 0)
    step(0, 0, b=False, c=False)
    sends(2, 0)
    sends(2, 1)
    relayed(0, 1)
    step(1, 1, c=False)
    sends(3, 0)
    sends(3, 1)

    def four(z, _):
        t = 4 * z + 2

        @pl.when(z > 0)
        def _():
            both(scatter_1, z - 1)

        step(t, 0)
        relay(z + 1, 0)
        relay(z + 1, 1)
        step(t + 1, 1)
        relayed(z + 1, 0)
        relayed(z + 1, 1)

        @pl.when(z > 0)
        def _():
            both(scatter_2, z - 1)

        @pl.when(z > 1)
        def _():
            both(scatter_3, z - 2)

        step(t + 2, 0)
        step(t + 3, 1)
        return 0

    lax.fori_loop(0, HK - 1, four, 0)
    last = HK - 1
    both(scatter_1, last - 1)
    step(14, 0)
    step(15, 1)
    both(scatter_2, last - 1)
    both(scatter_3, last - 2)
    step(16, 0, a=False)
    t, par = PAIRS - 1, 1
    sums_done(t, par)
    for k in range(SPAN // BLK):
        value_terms(par, k)
    scatter_1(last, 1)
    for k in range(SPAN // BLK):
        rows = key_terms(t, par, k)
        acc[0, :, rows] += dot(qs[par], dsb[t, rows, :].T)
    scatter_1(last, 0)
    scatter_2(last, 1)
    grad_queries(0)
    scatter_2(last, 0)
    grad_queries(1)
    both(scatter_3, last - 1)
    grad_queries(2)
    grad_queries(3)
    both(scatter_3, last)

    for h in range(HK):
        for w in range(2):
            x = seven(h, w)
            pltpu.make_async_copy(x, x, ag_send.at[h, w]).wait()
            y = kv.at[h, w, mine, :]
            remote(y, y, rl_send.at[h, w], rl_recv.at[h, w], sibling).wait_send()
            swap(h, w).wait_send()
            x = land.at[h, w]
            pltpu.make_async_copy(x, x, sc_send.at[h, w]).wait()


def publish(*refs):
    n = len(refs) // 2
    copies = [pltpu.make_async_copy(refs[i], refs[n + i], refs[-1].at[i]) for i in range(n)]
    for c in copies:
        c.start()
    for c in copies:
        c.wait()


def shards(queries, keys_resp, values_resp, keys_prompt, values_prompt, grad_out, resp_len):
    vm = pltpu.VMEM
    dma = pltpu.SemaphoreType.DMA
    wide = HK * D
    hbm = pl.BlockSpec(memory_space=pl.ANY)
    outs = pl.pallas_call(
        kernel,
        out_shape=(
            vm((ROWS, HK * G * D), BF),
            vm((ROWS, wide), BF),
            vm((ROWS, wide), BF),
            vm((SHARD, wide), BF),
            vm((SHARD, wide), BF),
        ),
        in_specs=[hbm] * 6 + [pl.BlockSpec(memory_space=pltpu.SMEM)],
        out_specs=(pl.BlockSpec(memory_space=vm),) * 5,
        scratch_shapes=[
            vm((HK, 2, SPAN, D), BF),
            vm((SPAN, W), F32), vm((SPAN, W), F32),
            vm((SPAN, W), F32), vm((SPAN, W), F32),
            vm((SPAN, W), BF), vm((SPAN, W), BF),
            vm((PAIRS, SPAN, W), BF),
            vm((2, 8, W), F32), vm((2, 8, W), F32), vm((2, 8, W), F32),
            vm((2, 8, W), F32), vm((2, 8, W), F32), vm((PAIRS, 8, W), F32),
            vm((HK * G, 2 * D, ROWS), BF), vm((HK * G, D, ROWS), BF),
            vm((D, SPAN), BF),
            vm((2, D, W), BF), vm((2, D, W), BF),
            vm((2, W, BLK), BF),
            vm((BLK, ROWS), F32),
            vm((2, D, SPAN), F32),
            vm((HK, 2, SPAN, D), BF),
            vm((HK, 2, HALF, D), BF),
            vm((HK, 2, CHIPS - 1, SHARD, D), BF),
            dma((9,)), dma((HK, 2, 2)),
            dma((HK, 2)), dma((HK, 2)), dma((HK, 2)), dma((HK, 2)),
            dma((HK, 2)), dma((HK, 2)), dma((HK, 2)), dma((HK, 2)),
        ],
        compiler_params=pltpu.CompilerParams(
            collective_id=0, has_side_effects=True, vmem_limit_bytes=56 * 2**20
        ),
    )(queries, grad_out, keys_resp, values_resp, keys_prompt, values_prompt, resp_len)
    return pl.pallas_call(
        publish,
        out_shape=tuple(jax.ShapeDtypeStruct(o.shape, o.dtype) for o in outs),
        in_specs=[pl.BlockSpec(memory_space=vm)] * 5,
        out_specs=(hbm,) * 5,
        scratch_shapes=[dma((5,))],
    )(*[pltpu.with_memory_space_constraint(o, vm) for o in outs])


def solution(mesh):
    rows = P(("grp", "seq"), None)
    return jax.shard_map(
        shards,
        mesh=mesh,
        in_specs=(rows,) * 6 + (P(("grp", "seq")),),
        out_specs=(rows,) * 5,
        check_vma=False,
    )
```

```python
import functools

import jax
import jax.numpy as jnp
from jax import lax
from jax.experimental import pallas as pl
from jax.experimental.pallas import tpu as pltpu
from jax.sharding import PartitionSpec as P

D = 128
HK = 4
G = 8
ROWS = 256
PROMPT = 1024
SPAN = PROMPT + ROWS
SHARD = 64
CHIPS = 8
HALF = CHIPS * SHARD
PAIRS = HK * G // 2
BLK = 256
SUB = 64
W = 2 * ROWS
SCALE = D**-0.5
LOG2E = 1.4426950408889634
NEG = -1e30
BF = jnp.bfloat16
F32 = jnp.float32


def dot(a, b):
    return lax.dot_general(a, b, (((1,), (0,)), ((), ())), preferred_element_type=F32)


def fold(x, op):
    return op(x.reshape(x.shape[0] // 8, 8, x.shape[1]), axis=0)


def lanes(i, n=1):
    return pl.ds(pl.multiple_of(i * D, D), n * D)


def kernel(
    q_hbm, g_hbm, kr_hbm, vr_hbm, kp_hbm, vp_hbm, len_ref,
    dq_ref, dkr_ref, dvr_ref, dkp_ref, dvp_ref,
    kv, s0, s1, d0, d1, p0, p1, dsb, mx, lx, dx, ms, ds_, rs, q_t, g_t, k_t, gs, qs,
    p_t, bias, acc, part, sib, land,
    in_sem, own_sem, ag_send, ag_recv, rl_send, rl_recv, sx_send, sx_recv, sc_send, sc_recv,
):
    s_buf, d_buf, p_buf = [s0, s1], [d0, d1], [p0, p1]
    me = lax.axis_index("seq")
    core, chip = lax.rem(me, 2), me // 2
    sibling = me + 1 - 2 * core

    def peer(o):
        return 2 * lax.rem(chip + o, CHIPS) + core

    def remote(src, dst, send, recv, to):
        return pltpu.make_async_remote_copy(
            src_ref=src, dst_ref=dst, send_sem=send, recv_sem=recv,
            device_id={"seq": to}, device_id_type=pl.DeviceIdType.MESH,
        )

    own = pl.ds(pl.multiple_of(core * HALF + chip * SHARD, SHARD), SHARD)
    mine = pl.ds(pl.multiple_of(core * HALF, HALF), HALF)
    theirs = pl.ds(pl.multiple_of((1 - core) * HALF, HALF), HALF)

    own_copies = []
    for h in range(HK):
        for w, (p_hbm, r_hbm) in enumerate(((kp_hbm, kr_hbm), (vp_hbm, vr_hbm))):
            col = pl.ds(h * D, D)
            c = pltpu.make_async_copy(p_hbm.at[:, col], kv.at[h, w, own, :], own_sem.at[h, w, 0])
            c.start()
            r = pltpu.make_async_copy(r_hbm.at[:, col], kv.at[h, w, pl.ds(PROMPT, ROWS), :], own_sem.at[h, w, 1])
            r.start()
            own_copies.append((c, r))
    q_copy = pltpu.make_async_copy(q_hbm, dq_ref, in_sem.at[0])
    q_copy.start()
    g_copies = []
    for j in range(HK * G * D // W):
        to = dsb.at[PAIRS - 2 + j // 4, pl.ds(j % 4 * ROWS, ROWS), :]
        g_copies.append(pltpu.make_async_copy(g_hbm.at[:, pl.ds(j * W, W)], to, in_sem.at[1 + j]))
        g_copies[-1].start()

    barrier = pltpu.get_barrier_semaphore()
    for o in range(1, CHIPS):
        pl.semaphore_signal(barrier, inc=1, device_id={"seq": peer(o)}, device_id_type=pl.DeviceIdType.MESH)
    pl.semaphore_signal(barrier, inc=1, device_id={"seq": sibling}, device_id_type=pl.DeviceIdType.MESH)
    pl.semaphore_wait(barrier, CHIPS)

    def sends(h, w):
        blk = kv.at[h, w, own, :]
        for o in range(1, CHIPS):
            remote(blk, blk, ag_send.at[h, w], ag_recv.at[h, w], peer(o)).start()

    def seven(h, w):
        return kv.at[h, w, pl.ds(0, (CHIPS - 1) * SHARD), :]

    def relay(h, w):
        x = seven(h, w)
        pltpu.make_async_copy(x, x, ag_recv.at[h, w]).wait()
        y = kv.at[h, w, mine, :]
        remote(y, y, rl_send.at[h, w], rl_recv.at[h, w], sibling).start()

    def relayed(h, w):
        y = kv.at[h, w, theirs, :]
        remote(y, y, rl_send.at[h, w], rl_recv.at[h, w], sibling).wait_recv()

    own_copies[0][0].wait()
    sends(0, 0)
    own_copies[1][0].wait()
    sends(0, 1)
    for c, _ in own_copies[2:]:
        c.wait()

    q_copy.wait()
    for c in g_copies:
        c.wait()
    live = lax.broadcasted_iota(jnp.int32, (D, ROWS), 1) < len_ref[0]

    def prep(i, _):
        qt = dq_ref[:, lanes(i)].T.astype(F32) * F32(SCALE * LOG2E)
        high = qt.astype(BF)
        q_t[i, 0:D, :] = high
        q_t[i, D : 2 * D, :] = (qt - high.astype(F32)).astype(BF)
        from_row = pl.ds(pl.multiple_of(i // 4 % 4 * ROWS, ROWS), ROWS)
        gt = dsb[PAIRS - 2 + i // 16, from_row, lanes(i % 4)].T.astype(F32)
        g_t[i] = jnp.where(live, gt, 0.0).astype(BF)
        return 0

    def prep_four(i, _):
        for u in range(4):
            prep(4 * i + u, 0)
        return 0

    acc[...] = jnp.zeros(acc.shape, F32)
    key = lax.broadcasted_iota(jnp.int32, (BLK, ROWS), 0)
    row = lax.broadcasted_iota(jnp.int32, (BLK, ROWS), 1)
    bias[...] = jnp.where(key <= row, 0.0, NEG).astype(F32)
    mx[...] = jnp.full(mx.shape, NEG, F32)
    lx[...] = jnp.zeros(lx.shape, F32)
    dx[...] = jnp.zeros(dx.shape, F32)
    for c, r in own_copies:
        r.wait()

    def stage_a(t, par, c):
        h, rows = t // 4, pl.ds(c * BLK, BLK)
        for u in range(2):
            ls = slice(u * ROWS, (u + 1) * ROWS)
            k = kv[h, 0, rows, :]
            s = dot(jnp.concatenate([k, k], axis=1), q_t[t * 2 + u])
            if c * BLK >= PROMPT:
                s = s + bias[...]
            s_buf[par][rows, ls] = s
            mx[par, :, ls] = jnp.maximum(mx[par, :, ls], fold(s, jnp.max))

    def stage_b(t, par, c):
        h, rows = t // 4, pl.ds(c * BLK, BLK)
        for u in range(2):
            ls = slice(u * ROWS, (u + 1) * ROWS)
            d = dot(kv[h, 1, rows, :], g_t[t * 2 + u])
            top, l_sum, d_sum = ms[par, 0:1, ls], lx[par, :, ls], dx[par, :, ls]
            for i in range(0, BLK, SUB):
                sub = pl.ds(c * BLK + i, SUB)
                p = jnp.exp2(s_buf[par][sub, ls] - top)
                l_sum += fold(p, jnp.sum)
                p_buf[par][sub, ls] = p.astype(BF)
                d_buf[par][sub, ls] = d[i : i + SUB]
                d_sum += fold(p * d[i : i + SUB], jnp.sum)
            lx[par, :, ls] = l_sum
            dx[par, :, ls] = d_sum

    def value_terms(par, c):
        rows = pl.ds(c * BLK, BLK)
        p_t[c % 2] = p_buf[par][rows, :].T
        acc[1, :, rows] += dot(gs[par], p_t[c % 2])

    def key_terms(t, par, c):
        rows = pl.ds(c * BLK, BLK)
        for i in range(0, BLK, SUB):
            sub = pl.ds(c * BLK + i, SUB)
            for u in range(2):
                ls = slice(u * ROWS, (u + 1) * ROWS)
                ds = (d_buf[par][sub, ls] - ds_[par, 0:1, ls]).astype(BF)
                dsb[t, sub, ls] = p_buf[par][sub, ls] * ds
        return rows

    def stage_c(t, par, c):
        rows = key_terms(t, par, c)
        value_terms(par, c)
        acc[0, :, rows] += dot(qs[par], dsb[t, rows, :].T)

    def max_done(par):
        m = jnp.max(mx[par], axis=0, keepdims=True)
        ms[par] = jnp.broadcast_to(m, (8, W))
        mx[par] = jnp.full((8, W), NEG, F32)

    def sums_done(t, par):
        r = 1.0 / jnp.sum(lx[par], axis=0, keepdims=True)
        ds_[par] = jnp.broadcast_to(jnp.sum(dx[par], axis=0, keepdims=True) * r, (8, W))
        rs[t] = jnp.broadcast_to(r * F32(SCALE), (8, W))
        lx[par] = jnp.zeros((8, W), F32)
        dx[par] = jnp.zeros((8, W), F32)
        for u in range(2):
            ls = slice(u * ROWS, (u + 1) * ROWS)
            gs[par, :, ls] = (g_t[t * 2 + u].astype(F32) * r[:, ls]).astype(BF)
            q = q_t[t * 2 + u, 0:D, :].astype(F32) + q_t[t * 2 + u, D : 2 * D, :].astype(F32)
            qs[par, :, ls] = (q * r[:, ls]).astype(BF)

    def grad_queries(h):
        k_t[...] = kv[h, 0].T
        for j in range(PAIRS // HK):
            t = h * (PAIRS // HK) + j
            x = dot(k_t[...], dsb[t]) * rs[t, 0:1, :]
            for u in range(2):
                dq_ref[:, lanes(2 * t + u)] = x[:, u * ROWS : (u + 1) * ROWS].astype(BF).T

    def step(t, par, a=True, b=True, c=True):
        if c:
            sums_done(t - 2, par)
        if b:
            max_done(1 - par)
        for k in range(SPAN // BLK):
            if a:
                stage_a(t, par, k)
            if b:
                stage_b(t - 1, 1 - par, k)
            if c:
                stage_c(t - 2, par, k)

    def swap(h, w):
        return remote(part.at[h, w, theirs, :], sib.at[h, w], sx_send.at[h, w], sx_recv.at[h, w], sibling)

    def scatter_1(h, w):
        x = acc[w] * F32(1 / LOG2E) if w == 0 else acc[w]
        part[h, w] = x.astype(BF).T
        acc[w] = jnp.zeros(acc.shape[1:], F32)
        swap(h, w).start()
        out = (dkr_ref, dvr_ref)[w]
        out[:, lanes(h)] = part[h, w, PROMPT:, :]

    def scatter_2(h, w):
        swap(h, w).wait_recv()
        part[h, w, mine, :] = (part[h, w, mine, :].astype(F32) + sib[h, w].astype(F32)).astype(BF)
        for o in range(1, CHIPS):
            to = lax.rem(chip + o, CHIPS)
            rows = pl.ds(pl.multiple_of(core * HALF + to * SHARD, SHARD), SHARD)
            remote(
                part.at[h, w, rows, :], land.at[h, w, CHIPS - 1 - o], sc_send.at[h, w], sc_recv.at[h, w], peer(o)
            ).start()

    def scatter_3(h, w):
        x = land.at[h, w]
        pltpu.make_async_copy(x, x, sc_recv.at[h, w]).wait()
        total = part[h, w, own, :].astype(F32)
        for o in range(CHIPS - 1):
            total = total + land[h, w, o].astype(F32)
        out = (dkp_ref, dvp_ref)[w]
        out[:, lanes(h)] = total.astype(BF)

    def both(f, h):
        f(h, 1)
        f(h, 0)

    half = HK * G // 8
    sends(1, 0)
    sends(1, 1)
    lax.fori_loop(0, half, prep_four, 0)
    relay(0, 0)
    sends(2, 0)
    sends(2, 1)
    lax.fori_loop(half, 2 * half, prep_four, 0)
    relay(0, 1)
    sends(3, 0)
    sends(3, 1)
    relayed(0, 0)
    step(0, 0, b=False, c=False)
    relayed(0, 1)
    step(1, 1, c=False)

    def four(z, _):
        t = 4 * z + 2

        @pl.when(z > 0)
        def _():
            both(scatter_1, z - 1)

        step(t, 0)
        relay(z + 1, 0)
        relay(z + 1, 1)
        step(t + 1, 1)
        relayed(z + 1, 0)
        relayed(z + 1, 1)

        @pl.when(z > 0)
        def _():
            both(scatter_2, z - 1)

        @pl.when(z > 1)
        def _():
            both(scatter_3, z - 2)

        step(t + 2, 0)
        step(t + 3, 1)
        return 0

    lax.fori_loop(0, HK - 1, four, 0)
    last = HK - 1
    both(scatter_1, last - 1)
    step(14, 0)
    step(15, 1)
    both(scatter_2, last - 1)
    both(scatter_3, last - 2)
    step(16, 0, a=False)
    t, par = PAIRS - 1, 1
    sums_done(t, par)
    for k in range(SPAN // BLK):
        value_terms(par, k)
    scatter_1(last, 1)
    for k in range(SPAN // BLK):
        rows = key_terms(t, par, k)
        acc[0, :, rows] += dot(qs[par], dsb[t, rows, :].T)
    scatter_1(last, 0)
    scatter_2(last, 1)
    grad_queries(0)
    scatter_2(last, 0)
    grad_queries(1)
    both(scatter_3, last - 1)
    grad_queries(2)
    grad_queries(3)
    both(scatter_3, last)

    for h in range(HK):
        for w in range(2):
            x = seven(h, w)
            pltpu.make_async_copy(x, x, ag_send.at[h, w]).wait()
            y = kv.at[h, w, mine, :]
            remote(y, y, rl_send.at[h, w], rl_recv.at[h, w], sibling).wait_send()
            swap(h, w).wait_send()
            x = land.at[h, w]
            pltpu.make_async_copy(x, x, sc_send.at[h, w]).wait()


def publish(*refs):
    n = len(refs) // 2
    copies = [pltpu.make_async_copy(refs[i], refs[n + i], refs[-1].at[i]) for i in range(n)]
    for c in copies:
        c.start()
    for c in copies:
        c.wait()


def shards(queries, keys_resp, values_resp, keys_prompt, values_prompt, grad_out, resp_len):
    vm = pltpu.VMEM
    dma = pltpu.SemaphoreType.DMA
    wide = HK * D
    hbm = pl.BlockSpec(memory_space=pl.ANY)
    outs = pl.pallas_call(
        kernel,
        out_shape=(
            vm((ROWS, HK * G * D), BF),
            vm((ROWS, wide), BF),
            vm((ROWS, wide), BF),
            vm((SHARD, wide), BF),
            vm((SHARD, wide), BF),
        ),
        in_specs=[hbm] * 6 + [pl.BlockSpec(memory_space=pltpu.SMEM)],
        out_specs=(pl.BlockSpec(memory_space=vm),) * 5,
        scratch_shapes=[
            vm((HK, 2, SPAN, D), BF),
            vm((SPAN, W), F32), vm((SPAN, W), F32),
            vm((SPAN, W), F32), vm((SPAN, W), F32),
            vm((SPAN, W), BF), vm((SPAN, W), BF),
            vm((PAIRS, SPAN, W), BF),
            vm((2, 8, W), F32), vm((2, 8, W), F32), vm((2, 8, W), F32),
            vm((2, 8, W), F32), vm((2, 8, W), F32), vm((PAIRS, 8, W), F32),
            vm((HK * G, 2 * D, ROWS), BF), vm((HK * G, D, ROWS), BF),
            vm((D, SPAN), BF),
            vm((2, D, W), BF), vm((2, D, W), BF),
            vm((2, W, BLK), BF),
            vm((BLK, ROWS), F32),
            vm((2, D, SPAN), F32),
            vm((HK, 2, SPAN, D), BF),
            vm((HK, 2, HALF, D), BF),
            vm((HK, 2, CHIPS - 1, SHARD, D), BF),
            dma((9,)), dma((HK, 2, 2)),
            dma((HK, 2)), dma((HK, 2)), dma((HK, 2)), dma((HK, 2)),
            dma((HK, 2)), dma((HK, 2)), dma((HK, 2)), dma((HK, 2)),
        ],
        compiler_params=pltpu.CompilerParams(
            collective_id=0, has_side_effects=True, vmem_limit_bytes=56 * 2**20
        ),
    )(queries, grad_out, keys_resp, values_resp, keys_prompt, values_prompt, resp_len)
    return pl.pallas_call(
        publish,
        out_shape=tuple(jax.ShapeDtypeStruct(o.shape, o.dtype) for o in outs),
        in_specs=[pl.BlockSpec(memory_space=vm)] * 5,
        out_specs=(hbm,) * 5,
        scratch_shapes=[dma((5,))],
    )(*[pltpu.with_memory_space_constraint(o, vm) for o in outs])


def solution(mesh):
    rows = P(("grp", "seq"), None)
    return jax.shard_map(
        shards,
        mesh=mesh,
        in_specs=(rows,) * 6 + (P(("grp", "seq")),),
        out_specs=(rows,) * 5,
        check_vma=False,
    )
```
